128 devices in a mesh: prompts: 8 (over y, core), units: 16 (over x, z).
Axes of the slice: x: 4, y: 4, z: 4, core: 2. Of those that a mesh axis runs over, the one named last changes fastest.
Arguments:
- hidden_acts: bfloat16 [32, 2048, 14336], P('prompts', None, 'units'), may hold values from -6 to 6
- out_grads: bfloat16 [32, 2048, 4096], P('prompts', None, 'units'), may hold values from -6 to 6
- proj_in: bfloat16 [14336, 64], P('units'), may hold values from -0.29231698 to 0.29231698
- proj_out: bfloat16 [4096, 64], P('units'), may hold values from -0.09375 to 0.09375
- lengths: int32 [32], P('prompts'), may hold values from 256 to 2048
- val_grads: float32 [512, 4096], P('prompts', 'units'), may hold values from -6 to 6
Outputs:
- scores: float32 [32, 512], P('prompts')
The draws below stay inside these ranges and needn't reach their ends.
All inputs are finite; a program needn't handle non-finite values.
Results may differ from the reference program's by a relative error of at most 0.0003.
Values sent between devices are 32-bit elements; how exact they have to be, the bound alone decides.
No kernel may reach another device: no remote copies, remote signals or barrier semaphores. Data moves between devices by JAX's collectives and lax.ppermute only.
A program may use at most 128 MiB of HBM per device.

```python
import jax
import jax.numpy as jnp
from jax import lax

D = 4096
FF = 14336
RANK = 64
LEN = 2048
TRAIN = 32
VAL = 512
FEAT = 4096


def draw_proj_in(key, part):
    first, second = jax.random.split(key)
    base = jnp.clip(jax.random.normal(first, (FF, RANK), jnp.float32), -6.0, 6.0)
    jitter = jax.random.uniform(second, (RANK,), jnp.float32, -0.5, 0.5)
    column = 10.0 ** ((jnp.arange(RANK, dtype=jnp.float32) + jitter) / RANK)
    return (base * column[None, :] / jnp.sqrt(jnp.float32(FF) * 3.0)).astype(jnp.bfloat16)


def place_ends(array, rng, smallest, top_value):
    extent = array.shape
    index_at = [jax.random.randint(jax.random.fold_in(rng, axis), (), 0, extent[axis]) for axis in range(len(extent))]
    array = array.at[tuple(index_at)].set(smallest)
    longest = extent.index(max(extent))
    index_at[longest] = (index_at[longest] + 1) % extent[longest]
    return array.at[tuple(index_at)].set(top_value)


def shard_levels(rng, shape, shards, smallest, largest):
    def one(position, parts):
        draws = jax.random.uniform(jax.random.fold_in(jax.random.fold_in(rng, 6), position), (parts,), jnp.float32, smallest / len(shards), largest / len(shards))
        return jnp.repeat(jnp.exp(draws), shape[position] // parts).reshape((-1,) + (1,) * (len(shape) - position - 1))

    level = one(*shards[0])
    for cut in shards[1:]:
        level = level * one(*cut)
    return level


def noise(rng, shape, deviation, bound, shards=(), kind=jnp.bfloat16):
    factor_of = shard_levels(rng, shape, shards, -0.22, 0.18) if shards else 1.0
    drawn = jax.random.normal(rng, shape, jnp.float32) * deviation * factor_of
    return jnp.minimum(jnp.maximum(drawn, -bound), bound).astype(kind)


def setup_inputs(seed: int = 0) -> dict:
    seeds = jax.random.split(jax.random.key(seed), 7)
    hidden_acts = noise(seeds[0], (TRAIN, LEN, FF), 1.0, 6.0, ((0, 8), (2, 16)))
    out_grads = noise(seeds[1], (TRAIN, LEN, D), 1.0, 6.0, ((0, 8), (2, 16)))
    proj_in = draw_proj_in(jax.random.fold_in(seeds[6], 71), 0)
    proj_out = noise(seeds[3], (D, RANK), D ** -0.5, 0.09375, ((0, 16),))
    lengths = place_ends(jax.random.randint(seeds[4], (TRAIN,), LEN // 8, LEN + 1), jax.random.fold_in(seeds[4], 1), LEN // 8, LEN).astype(jnp.int32)
    val_grads = noise(seeds[5], (VAL, FEAT), 1.0, 6.0, ((0, 8), (1, 16)), jnp.float32)
    return {"hidden_acts": hidden_acts, "out_grads": out_grads, "proj_in": proj_in, "proj_out": proj_out, "lengths": lengths, "val_grads": val_grads}


def one_prompt(item, proj_in, proj_out):
    acts, grads_out, length = item
    inner = jnp.dot(acts, proj_in, preferred_element_type=jnp.float32)
    outer = jnp.dot(grads_out, proj_out, preferred_element_type=jnp.float32)
    valid = (jnp.arange(acts.shape[0], dtype=jnp.int32) < length).astype(jnp.float32)
    inner = inner * valid[:, None]
    full = jnp.dot(inner.T, outer, precision=lax.Precision.HIGHEST, preferred_element_type=jnp.float32)
    return full.reshape(-1)

def reference(hidden_acts, out_grads, proj_in, proj_out, lengths, val_grads):
    grads = lax.map(lambda item: one_prompt(item, proj_in, proj_out), (hidden_acts, out_grads, lengths))
    dots = jnp.dot(grads, val_grads.T, precision=lax.Precision.HIGHEST, preferred_element_type=jnp.float32)
    squares = lax.optimization_barrier(jnp.sum(grads * grads, axis=1))
    return dots / jnp.sqrt(squares + 1e-06)[:, None]
```

```python
import jax
import jax.numpy as jnp
from jax import lax
from jax.experimental import pallas as pl
from jax.experimental.pallas import tpu as pltpu
from jax.sharding import PartitionSpec as P

SIDE = 4
PIECES = 2 * SIDE * SIDE
BLOCK_SIZES = (64, 96, 112, 128, 144, 160, 176, 192, 208, 224, 256)


def block_info(scal, tb, m):
    first = 0
    prompt = 0
    start = 0
    for p in range(4):
        count = (scal[p] + (tb - 1)) // tb
        here = m >= first
        prompt = jnp.where(here, p, prompt)
        start = jnp.where(here, first, start)
        first = first + count
    block = m - start
    length = jnp.where(prompt == 0, scal[0], jnp.where(prompt == 1, scal[1], jnp.where(prompt == 2, scal[2], scal[3])))
    inside = m < first
    rows = jnp.where(inside, jnp.clip(length - block * tb, 0, tb), 0)
    block = jnp.where(inside, block, 0)
    return prompt, block, rows


def packed_index(scal, h, j, k):
    first = lax.rem(jnp.where(h == 0, scal[4], scal[5]) + j, SIDE)
    second = lax.rem(jnp.where(h == 0, scal[5], scal[4]) + k, SIDE)
    return h * (SIDE * SIDE) + first * SIDE + second


def project_kernel(j, tb, scal, acts, grads, w_in, w_out, first_ref, second_ref):
    h, k = pl.program_id(0), pl.program_id(1)
    _, _, rows = block_info(scal, tb, packed_index(scal, h, j, k))
    dims = (((1,), (1,)), ((), ()))
    inner = lax.dot_general(acts[0], w_in[...], dims, preferred_element_type=jnp.float32)
    outer = lax.dot_general(grads[0], w_out[...], dims, preferred_element_type=jnp.float32)
    both = jnp.concatenate([inner, outer], axis=1)
    both = jnp.where(lax.broadcasted_iota(jnp.int32, both.shape, 0) < rows, both, 0.0)

    @pl.when(h == 0)
    def _():
        first_ref[0] = both

    @pl.when(h == 1)
    def _():
        second_ref[0] = both


def project_slot(j, tb, scal, acts, grads, w_in, w_out):
    def source(h, k, s):
        prompt, block, _ = block_info(s, tb, packed_index(s, h, j, k))
        return prompt, block, 0

    units, width = acts.shape[2], grads.shape[2]
    whole = lambda h, k, s: (0, 0)
    out = jax.ShapeDtypeStruct((SIDE, tb, 128), jnp.float32)
    return pl.pallas_call(
        lambda *refs: project_kernel(j, tb, *refs),
        grid_spec=pltpu.PrefetchScalarGridSpec(
            num_scalar_prefetch=1,
            grid=(2, SIDE),
            in_specs=[
                pl.BlockSpec((1, tb, units), source),
                pl.BlockSpec((1, tb, width), source),
                pl.BlockSpec(w_in.shape, whole),
                pl.BlockSpec(w_out.shape, whole),
            ],
            out_specs=[
                pl.BlockSpec((1, tb, 128), lambda h, k, s: (jnp.where(h == 0, k, SIDE - 1), 0, 0)),
                pl.BlockSpec((1, tb, 128), lambda h, k, s: (jnp.where(h == 1, k, 0), 0, 0)),
            ],
        ),
        out_shape=[out, out],
        compiler_params=pltpu.CompilerParams(vmem_limit_bytes=24 * 1024 * 1024),
        cost_estimate=pl.CostEstimate(
            flops=2 * 2 * SIDE * tb * (units + width) * 256,
            bytes_accessed=2 * SIDE * tb * ((units + width) * 2 + 512),
            transcendentals=0,
        ),
    )(scal, acts, grads, w_in, w_out)


def along(axis, step):
    pairs = []
    for x in range(SIDE):
        for z in range(SIDE):
            if axis == "x":
                pairs.append((x * SIDE + z, (x + step) % SIDE * SIDE + z))
            else:
                pairs.append((x * SIDE + z, x * SIDE + (z + step) % SIDE))
    return pairs


def send(value, axis, step):
    return lax.ppermute(value, "units", along(axis, step))


def reduce_blocks(tb, scal, acts, grads, w_in, w_out):
    got = {"x": [], "z": []}
    for j in (2, 1, 3):
        first, second = project_slot(j, tb, scal, acts, grads, w_in, w_out)
        got["x"].append(send(first, "x", j))
        got["z"].append(send(second, "z", j))
    first, second = project_slot(0, tb, scal, acts, grads, w_in, w_out)
    total_x = first + sum(got["x"])
    total_z = second + sum(got["z"])
    final_x = [send(total_x[k], "z", k) for k in (2, 1, 3)]
    final_z = [send(total_z[k], "x", k) for k in (2, 1, 3)]
    rows_x = total_x[0] + sum(final_x)
    rows_z = total_z[0] + sum(final_z)
    rows = jnp.stack([rows_x, rows_z])
    here = jnp.stack([packed_index(scal, h, 0, 0) for h in (0, 1)])
    prompt, _, _ = block_info(scal, tb, here)
    pick = (prompt[:, None] == jnp.arange(4, dtype=jnp.int32)[None, :]).astype(jnp.float32)
    each = jnp.einsum("bti,btj->bij", rows[:, :, :64], rows[:, :, 64:], precision=lax.Precision.HIGHEST)
    return jnp.sum(pick[:, :, None, None] * each[:, None], axis=0)


def per_device(hidden_acts, out_grads, proj_in, proj_out, lengths, val_grads):
    place = lax.axis_index("units").astype(jnp.int32)
    scal = jnp.concatenate([lengths, jnp.stack([place // SIDE, place % SIDE])])
    w_in, w_out = proj_in.T, proj_out.T
    branch = jnp.int32(0)
    for tb in BLOCK_SIZES[:-1]:
        blocks = jnp.sum((lengths + (tb - 1)) // tb)
        branch = branch + (blocks > PIECES).astype(jnp.int32)
    partial = lax.switch(
        branch,
        [lambda *ops, tb=tb: reduce_blocks(tb, *ops) for tb in BLOCK_SIZES],
        scal, hidden_acts, out_grads, w_in, w_out,
    )
    val_all = lax.all_gather(val_grads, "prompts", axis=0, tiled=True)
    shards = partial.reshape(4, 16, 256).transpose(1, 0, 2)
    grads = jnp.sum(lax.all_to_all(shards, "units", 0, 0, tiled=True), axis=0)
    dots = jnp.einsum("pf,vf->pv", grads, val_all, precision=lax.Precision.HIGHEST)
    squares = jnp.sum(grads * grads, axis=1)
    packed = jnp.concatenate([dots, jnp.broadcast_to(squares[:, None], (4, 128))], axis=1)
    spread = jnp.broadcast_to(packed[None], (16,) + packed.shape)
    sums = jnp.sum(lax.all_to_all(spread, "units", 0, 0, tiled=True), axis=0)
    return sums[:, :512] / jnp.sqrt(sums[:, 512:513] + 1e-06)


def solution(mesh):
    in_specs = (
        P("prompts", None, "units"),
        P("prompts", None, "units"),
        P("units", None),
        P("units", None),
        P("prompts"),
        P("prompts", "units"),
    )
    return jax.shard_map(
        per_device, mesh=mesh, in_specs=in_specs, out_specs=P("prompts", None), check_vma=False
    )
```

```python
import jax
import jax.numpy as jnp
from jax import lax
from jax.experimental import pallas as pl
from jax.experimental.pallas import tpu as pltpu
from jax.sharding import PartitionSpec as P

SIDE = 4
PIECES = 2 * SIDE * SIDE
SLOTS = 2048
GROUP = 4
BLOCK_SIZES = (160, 192, 224, 256)


def blocks_of(scal, p, tb):
    return (scal[p] + (tb - 1)) // tb


def block_info(scal, tb, m):
    second = blocks_of(scal, 0, tb)
    third = second + blocks_of(scal, 1, tb)
    fourth = third + blocks_of(scal, 2, tb)
    end = fourth + blocks_of(scal, 3, tb)
    prompt = (m >= second).astype(jnp.int32) + (m >= third).astype(jnp.int32) + (m >= fourth).astype(jnp.int32)
    first = jnp.where(m >= fourth, fourth, jnp.where(m >= third, third, jnp.where(m >= second, second, 0)))
    token = (m - first) * tb
    inside = m < end
    token = jnp.where(inside, token, 0)
    start = jnp.minimum(token, SLOTS - tb)
    high = jnp.where(inside, scal[prompt] - start, 0)
    return prompt, pl.multiple_of(start, 16), token - start, high


def packed_index(scal, h, j, k):
    x, z = scal[4], scal[5]
    major = jnp.where(h == 0, x, z)
    minor = jnp.where(h == 0, z, x)
    return h * (SIDE * SIDE) + ((major + j) & 3) * SIDE + ((minor + k) & 3)


def plan_kernel(lengths, place, out):
    for p in range(4):
        out[p] = lengths[p]
    out[4] = place[0] >> 2
    out[5] = place[0] & 3
    branch = 0
    for tb in BLOCK_SIZES[:-1]:
        blocks = sum(blocks_of(lengths, p, tb) for p in range(4))
        branch = branch + (blocks > PIECES).astype(jnp.int32)
    out[6] = branch
    out[7] = 0


def project_kernel(tb, steps, scal, acts, grads, w_in, w_out, *refs):
    count = 2 * len(steps)
    outs = refs[:count]
    buf, w_buf, result, bounds, a_sem, g_sem, w_sem, r_sem = refs[count:]
    units = acts.shape[2]
    w_buf[...] = jnp.zeros_like(w_buf)
    weights = [
        pltpu.make_async_copy(w_in, w_buf.at[:64, :units], w_sem.at[0]),
        pltpu.make_async_copy(w_out, w_buf.at[64:, units:], w_sem.at[1]),
    ]
    for copy in weights:
        copy.start()

    def pair(n, k, prompt, start):
        rows = pl.ds(pl.multiple_of(k * tb, 16), tb)
        return (
            pltpu.make_async_copy(acts.at[prompt, pl.ds(start, tb)], buf.at[n, rows, :units], a_sem.at[n]),
            pltpu.make_async_copy(grads.at[prompt, pl.ds(start, tb)], buf.at[n, rows, units:], g_sem.at[n]),
        )

    def fetch(i, _):
        n, k = i >> 2, i & 3
        j = steps[-1]
        for place, step in enumerate(steps[:-1]):
            j = jnp.where(n >> 1 == place, step, j)
        prompt, start, low, high = block_info(scal, tb, packed_index(scal, n & 1, j, k))
        bounds[i, 0] = low
        bounds[i, 1] = high
        for copy in pair(n, k, prompt, start):
            copy.start()
        return 0

    lax.fori_loop(0, count * SIDE, fetch, 0)
    for copy in weights:
        copy.wait()
    row = lax.broadcasted_iota(jnp.int32, (tb, 128), 0)

    def hand_over(n, act):
        for q in range(count):
            @pl.when(n == q)
            def _():
                act(pltpu.make_async_copy(result.at[q & 1], outs[q], r_sem.at[q & 1]))

    def compute(n, _):
        for k in range(SIDE):
            for copy in pair(n, k, 0, 0):
                copy.wait()
        hand_over(n - 2, lambda copy: copy.wait())
        for c in range(SIDE // GROUP):
            both = lax.dot_general(
                buf[n, c * GROUP * tb : (c + 1) * GROUP * tb], w_buf[...], (((1,), (1,)), ((), ())),
                preferred_element_type=jnp.float32,
            )
            for k in range(GROUP):
                at = c * GROUP + k
                keep = (row >= bounds[n * SIDE + at, 0]) & (row < bounds[n * SIDE + at, 1])
                result[n & 1, at] = jnp.where(keep, both[k * tb : (k + 1) * tb], 0.0)
        hand_over(n, lambda copy: copy.start())
        return 0

    lax.fori_loop(0, count, compute, 0)
    for q in range(count - 2, count):
        pltpu.make_async_copy(result.at[q & 1], outs[q], r_sem.at[q & 1]).wait()


def project(tb, steps, scal, acts, grads, w_in, w_out):
    units, width = acts.shape[2], grads.shape[2]
    count = 2 * len(steps)
    rows = count * SIDE * tb
    return pl.pallas_call(
        lambda *refs: project_kernel(tb, steps, *refs),
        in_specs=[pl.BlockSpec(memory_space=pltpu.SMEM)] + [pl.BlockSpec(memory_space=pl.ANY)] * 4,
        out_specs=[pl.BlockSpec(memory_space=pltpu.VMEM)] * count,
        out_shape=[jax.ShapeDtypeStruct((SIDE, tb, 128), jnp.float32)] * count,
        scratch_shapes=[
            pltpu.VMEM((count, SIDE * tb, units + width), jnp.bfloat16),
            pltpu.VMEM((128, units + width), jnp.bfloat16),
            pltpu.VMEM((2, SIDE, tb, 128), jnp.float32),
            pltpu.SMEM((count * SIDE, 2), jnp.int32),
            pltpu.SemaphoreType.DMA((count,)),
            pltpu.SemaphoreType.DMA((count,)),
            pltpu.SemaphoreType.DMA((2,)),
            pltpu.SemaphoreType.DMA((2,)),
        ],
        compiler_params=pltpu.CompilerParams(vmem_limit_bytes=36 * 1024 * 1024),
        cost_estimate=pl.CostEstimate(
            flops=2 * rows * (units + width) * 256,
            bytes_accessed=rows * ((units + width) * 2 + 512),
            transcendentals=0,
        ),
    )(scal, acts, grads, w_in, w_out)


def outer_kernel(tb, scal, *refs):
    out = refs[-1]
    row = lax.broadcasted_iota(jnp.int32, (64, 64), 0)
    col = lax.broadcasted_iota(jnp.int32, (64, 64), 1)
    order = ((row & 15) * 4 + (row >> 4) == col).astype(jnp.float32)
    each, owner = [], []
    for h in range(2):
        a, b, c, d = (ref[...] for ref in refs[4 * h : 4 * h + 4])
        rows = (a + b) + (c + d)
        product = lax.dot_general(
            rows[:, :64], rows[:, 64:], (((0,), (0,)), ((), ())),
            precision=lax.Precision.HIGHEST, preferred_element_type=jnp.float32,
        )
        each.append(jnp.dot(order, product, precision=lax.Precision.HIGHEST, preferred_element_type=jnp.float32))
        owner.append(block_info(scal, tb, packed_index(scal, h, 0, 0))[0])
    for p in range(4):
        total = jnp.where(owner[0] == p, each[0], 0.0) + jnp.where(owner[1] == p, each[1], 0.0)
        for i in range(4):
            out[:, p, i * 64 : (i + 1) * 64] = total[i * 16 : (i + 1) * 16]


def along(axis, step):
    pairs = []
    for x in range(SIDE):
        for z in range(SIDE):
            if axis == "x":
                pairs.append((x * SIDE + z, (x + step) % SIDE * SIDE + z))
            else:
                pairs.append((x * SIDE + z, x * SIDE + (z + step) % SIDE))
    return pairs


def send(value, axis, step):
    return lax.ppermute(value, "units", along(axis, step))


def reduce_blocks(tb, scal, acts, grads, w_in, w_out):
    x2, z2 = project(tb, (2,), scal, acts, grads, w_in, w_out)
    got_x = [send(x2, "x", 2)]
    got_z = [send(z2, "z", 2)]
    x1, z1, x3, z3, x0, z0 = project(tb, (1, 3, 0), scal, acts, grads, w_in, w_out)
    got_x += [send(x1, "x", 1), send(x3, "x", 3)]
    got_z += [send(z1, "z", 1), send(z3, "z", 3)]
    total_x = x0 + sum(got_x)
    total_z = z0 + sum(got_z)
    final = []
    for total, axis in ((total_x, "z"), (total_z, "x")):
        final.append(total[0])
        final += [send(total[k], axis, k) for k in (2, 1, 3)]
    return pl.pallas_call(
        lambda *refs: outer_kernel(tb, *refs),
        in_specs=[pl.BlockSpec(memory_space=pltpu.SMEM)] + [pl.BlockSpec(memory_space=pltpu.VMEM)] * 8,
        out_specs=pl.BlockSpec(memory_space=pltpu.VMEM),
        out_shape=jax.ShapeDtypeStruct((16, 4, 256), jnp.float32),
    )(scal, *final)


def dots_kernel(received, pair_0, pair_1, pair_2, pair_3, out):
    grads = jnp.sum(received[...], axis=0)
    squares = jnp.sum(grads * grads, axis=1, keepdims=True)
    parts = []
    for pair in (pair_0, pair_1, pair_2, pair_3):
        parts.append(lax.dot_general(
            grads, pair[...], (((1,), (1,)), ((), ())),
            precision=lax.Precision.HIGHEST, preferred_element_type=jnp.float32,
        ))
    parts.append(jnp.broadcast_to(squares, (4, 128)))
    packed = jnp.concatenate(parts, axis=1)
    out[...] = jnp.broadcast_to(packed[None], out.shape)


def scores_kernel(group, received, out):
    sums = jnp.sum(received[...], axis=0)
    scale = jnp.sqrt(sums[:, 512:640] + 1e-06)
    y, core = group[0] >> 1, group[0] & 1
    for n in range(4):
        part = pltpu.roll(sums[:, n * 128 : (n + 1) * 128], core * 64, 1) / scale
        out[:, pl.ds(pl.multiple_of(((y - n) & 3) * 128, 128), 128)] = part


def per_device(hidden_acts, out_grads, proj_in, proj_out, lengths, val_grads):
    place = lax.axis_index("units").astype(jnp.int32).reshape(1)
    group = lax.axis_index("prompts").astype(jnp.int32).reshape(1)
    smem = pl.BlockSpec(memory_space=pltpu.SMEM)
    vmem = pl.BlockSpec(memory_space=pltpu.VMEM)
    other = lax.ppermute(val_grads, "prompts", [(n, n ^ 1) for n in range(8)])
    scal = pl.pallas_call(
        plan_kernel,
        in_specs=[smem] * 2,
        out_specs=smem,
        out_shape=jax.ShapeDtypeStruct((8,), jnp.int32),
    )(lengths, place)
    shards = lax.switch(
        scal[6],
        [lambda *ops, tb=tb: reduce_blocks(tb, *ops) for tb in BLOCK_SIZES],
        scal, hidden_acts, out_grads, proj_in.T, proj_out.T,
    )
    pairs = [jnp.concatenate([val_grads, other])]
    for step in (1, 3, 2):
        hops = [(2 * y + c, 2 * ((y + step) % 4) + c) for y in range(4) for c in range(2)]
        pairs.append(lax.ppermute(pairs[0], "prompts", hops))
    pairs = [pairs[0], pairs[1], pairs[3], pairs[2]]
    received = lax.all_to_all(shards, "units", 0, 0, tiled=True)
    packed = pl.pallas_call(
        dots_kernel,
        in_specs=[vmem] * 5,
        out_specs=vmem,
        out_shape=jax.ShapeDtypeStruct((16, 4, 640), jnp.float32),
    )(received, *pairs)
    return pl.pallas_call(
        scores_kernel,
        in_specs=[smem, vmem],
        out_specs=vmem,
        out_shape=jax.ShapeDtypeStruct((4, 512), jnp.float32),
    )(group, lax.all_to_all(packed, "units", 0, 0, tiled=True))


def solution(mesh):
    in_specs = (
        P("prompts", None, "units"),
        P("prompts", None, "units"),
        P("units", None),
        P("units", None),
        P("prompts"),
        P("prompts", "units"),
    )
    return jax.shard_map(
        per_device, mesh=mesh, in_specs=in_specs, out_specs=P("prompts", None), check_vma=False
    )
```

```python
import jax
import jax.numpy as jnp
from jax import lax
from jax.experimental import pallas as pl
from jax.experimental.pallas import tpu as pltpu
from jax.sharding import PartitionSpec as P

SIDE = 4
PIECES = 2 * SIDE * SIDE
SLOTS = 2048
GROUP = 4
BLOCK_SIZES = (160, 192, 224, 256)


def blocks_of(scal, p, tb):
    return (scal[p] + (tb - 1)) // tb


def block_info(scal, tb, m):
    second = blocks_of(scal, 0, tb)
    third = second + blocks_of(scal, 1, tb)
    fourth = third + blocks_of(scal, 2, tb)
    end = fourth + blocks_of(scal, 3, tb)
    prompt = (m >= second).astype(jnp.int32) + (m >= third).astype(jnp.int32) + (m >= fourth).astype(jnp.int32)
    first = jnp.where(m >= fourth, fourth, jnp.where(m >= third, third, jnp.where(m >= second, second, 0)))
    token = (m - first) * tb
    inside = m < end
    token = jnp.where(inside, token, 0)
    start = jnp.minimum(token, SLOTS - tb)
    high = jnp.where(inside, scal[prompt] - start, 0)
    return prompt, pl.multiple_of(start, 16), token - start, high


def packed_index(scal, h, j, k):
    x, z = scal[4], scal[5]
    major = jnp.where(h == 0, x, z)
    minor = jnp.where(h == 0, z, x)
    return h * (SIDE * SIDE) + ((major + j) & 3) * SIDE + ((minor + k) & 3)


def plan_kernel(lengths, place, out):
    for p in range(4):
        out[p] = lengths[p]
    out[4] = place[0] >> 2
    out[5] = place[0] & 3
    branch = 0
    for tb in BLOCK_SIZES[:-1]:
        blocks = sum(blocks_of(lengths, p, tb) for p in range(4))
        branch = branch + (blocks > PIECES).astype(jnp.int32)
    out[6] = branch
    out[7] = 0


def project_kernel(tb, steps, scal, acts, grads, w_in, w_out, *refs):
    count = 2 * len(steps)
    outs = refs[:count]
    buf, w_buf, result, bounds, a_sem, g_sem, w_sem, r_sem = refs[count:]
    units = acts.shape[2]
    w_buf[...] = jnp.zeros_like(w_buf)
    weights = [
        pltpu.make_async_copy(w_in, w_buf.at[:64, :units], w_sem.at[0]),
        pltpu.make_async_copy(w_out, w_buf.at[64:, units:], w_sem.at[1]),
    ]
    for copy in weights:
        copy.start()

    def pair(n, k, prompt, start):
        rows = pl.ds(pl.multiple_of(k * tb, 16), tb)
        return (
            pltpu.make_async_copy(acts.at[prompt, pl.ds(start, tb)], buf.at[n, rows, :units], a_sem.at[n]),
            pltpu.make_async_copy(grads.at[prompt, pl.ds(start, tb)], buf.at[n, rows, units:], g_sem.at[n]),
        )

    def fetch(i, _):
        n, k = i >> 2, i & 3
        j = steps[-1]
        for place, step in enumerate(steps[:-1]):
            j = jnp.where(n >> 1 == place, step, j)
        prompt, start, low, high = block_info(scal, tb, packed_index(scal, n & 1, j, k))
        bounds[i, 0] = low
        bounds[i, 1] = high
        for copy in pair(n, k, prompt, start):
            copy.start()
        return 0

    lax.fori_loop(0, count * SIDE, fetch, 0)
    for copy in weights:
        copy.wait()
    row = lax.broadcasted_iota(jnp.int32, (tb, 128), 0)

    def hand_over(n, act):
        for q in range(count):
            @pl.when(n == q)
            def _():
                act(pltpu.make_async_copy(result.at[q & 1], outs[q], r_sem.at[q & 1]))

    def compute(n, _):
        for k in range(SIDE):
            for copy in pair(n, k, 0, 0):
                copy.wait()
        hand_over(n - 2, lambda copy: copy.wait())
        for c in range(SIDE // GROUP):
            both = lax.dot_general(
                buf[n, c * GROUP * tb : (c + 1) * GROUP * tb], w_buf[...], (((1,), (1,)), ((), ())),
                preferred_element_type=jnp.float32,
            )
            for k in range(GROUP):
                at = c * GROUP + k
                keep = (row >= bounds[n * SIDE + at, 0]) & (row < bounds[n * SIDE + at, 1])
                result[n & 1, at] = jnp.where(keep, both[k * tb : (k + 1) * tb], 0.0)
        hand_over(n, lambda copy: copy.start())
        return 0

    lax.fori_loop(0, count, compute, 0)
    for q in range(count - 2, count):
        pltpu.make_async_copy(result.at[q & 1], outs[q], r_sem.at[q & 1]).wait()


def project(tb, steps, scal, acts, grads, w_in, w_out):
    units, width = acts.shape[2], grads.shape[2]
    count = 2 * len(steps)
    rows = count * SIDE * tb
    return pl.pallas_call(
        lambda *refs: project_kernel(tb, steps, *refs),
        in_specs=[pl.BlockSpec(memory_space=pltpu.SMEM)] + [pl.BlockSpec(memory_space=pl.ANY)] * 4,
        out_specs=[pl.BlockSpec(memory_space=pltpu.VMEM)] * count,
        out_shape=[jax.ShapeDtypeStruct((SIDE, tb, 128), jnp.float32)] * count,
        scratch_shapes=[
            pltpu.VMEM((count, SIDE * tb, units + width), jnp.bfloat16),
            pltpu.VMEM((128, units + width), jnp.bfloat16),
            pltpu.VMEM((2, SIDE, tb, 128), jnp.float32),
            pltpu.SMEM((count * SIDE, 2), jnp.int32),
            pltpu.SemaphoreType.DMA((count,)),
            pltpu.SemaphoreType.DMA((count,)),
            pltpu.SemaphoreType.DMA((2,)),
            pltpu.SemaphoreType.DMA((2,)),
        ],
        compiler_params=pltpu.CompilerParams(vmem_limit_bytes=36 * 1024 * 1024),
        cost_estimate=pl.CostEstimate(
            flops=2 * rows * (units + width) * 256,
            bytes_accessed=rows * ((units + width) * 2 + 512),
            transcendentals=0,
        ),
    )(scal, acts, grads, w_in, w_out)


def fetch_all(refs, sems):
    half = len(refs) // 2
    copies = [pltpu.make_async_copy(refs[n], refs[half + n], sems.at[n]) for n in range(half)]
    for copy in copies:
        copy.start()
    for copy in copies:
        copy.wait()
    return [ref[...] for ref in refs[half:]]


def call_fetching(kernel, out_shape, scalars, operands):
    def body(*refs):
        first, last = len(scalars), len(scalars) + len(operands)
        kernel(refs[:first], fetch_all(refs[first:last] + refs[last + 1 : -1], refs[-1]), refs[last])

    return pl.pallas_call(
        body,
        in_specs=[pl.BlockSpec(memory_space=pltpu.SMEM)] * len(scalars) + [pl.BlockSpec(memory_space=pl.ANY)] * len(operands),
        out_specs=pl.BlockSpec(memory_space=pltpu.VMEM),
        out_shape=jax.ShapeDtypeStruct(out_shape, jnp.float32),
        scratch_shapes=[pltpu.VMEM(v.shape, v.dtype) for v in operands] + [pltpu.SemaphoreType.DMA((len(operands),))],
        compiler_params=pltpu.CompilerParams(vmem_limit_bytes=12 * 1024 * 1024),
    )(*scalars, *operands)


def outer_kernel(tb, scalars, values, out):
    scal = scalars[0]
    row = lax.broadcasted_iota(jnp.int32, (64, 64), 0)
    col = lax.broadcasted_iota(jnp.int32, (64, 64), 1)
    order = ((row & 15) * 4 + (row >> 4) == col).astype(jnp.float32)
    each, owner = [], []
    for h in range(2):
        a, b, c, d = values[4 * h : 4 * h + 4]
        rows = (a + b) + (c + d)
        product = lax.dot_general(
            rows[:, :64], rows[:, 64:], (((0,), (0,)), ((), ())),
            precision=lax.Precision.HIGHEST, preferred_element_type=jnp.float32,
        )
        each.append(jnp.dot(order, product, precision=lax.Precision.HIGHEST, preferred_element_type=jnp.float32))
        owner.append(block_info(scal, tb, packed_index(scal, h, 0, 0))[0])
    for p in range(4):
        total = jnp.where(owner[0] == p, each[0], 0.0) + jnp.where(owner[1] == p, each[1], 0.0)
        for i in range(4):
            out[:, p, i * 64 : (i + 1) * 64] = total[i * 16 : (i + 1) * 16]


def along(axis, step):
    pairs = []
    for x in range(SIDE):
        for z in range(SIDE):
            if axis == "x":
                pairs.append((x * SIDE + z, (x + step) % SIDE * SIDE + z))
            else:
                pairs.append((x * SIDE + z, x * SIDE + (z + step) % SIDE))
    return pairs


def send(value, axis, step):
    return lax.ppermute(value, "units", along(axis, step))


def reduce_blocks(tb, scal, acts, grads, w_in, w_out):
    x2, z2 = project(tb, (2,), scal, acts, grads, w_in, w_out)
    from_x2, from_z2 = send(x2, "x", 2), send(z2, "z", 2)
    x1, z1, x3, z3, x0, z0 = project(tb, (1, 3, 0), scal, acts, grads, w_in, w_out)
    from_x1, from_z1 = send(x1, "x", 1), send(z1, "z", 1)
    sum_x, sum_z, x3, z3 = lax.optimization_barrier((x0 + from_x2, z0 + from_z2, x3, z3))
    total_x = sum_x + (from_x1 + send(x3, "x", 3))
    total_z = sum_z + (from_z1 + send(z3, "z", 3))
    final = []
    for total, axis in ((total_x, "z"), (total_z, "x")):
        final.append(total[0])
        final += [send(total[k], axis, k) for k in (2, 1, 3)]
    return call_fetching(lambda *refs: outer_kernel(tb, *refs), (16, 4, 256), [scal], final)


def pair_up(mine, other, _after):
    def body(mine_ref, other_ref, _, out, sems):
        copies = [
            pltpu.make_async_copy(mine_ref, out.at[:64], sems.at[0]),
            pltpu.make_async_copy(other_ref, out.at[64:], sems.at[1]),
        ]
        for copy in copies:
            copy.start()
        for copy in copies:
            copy.wait()

    return pl.pallas_call(
        body,
        in_specs=[pl.BlockSpec(memory_space=pl.ANY)] * 3,
        out_specs=pl.BlockSpec(memory_space=pl.ANY),
        out_shape=jax.ShapeDtypeStruct((128, mine.shape[1]), mine.dtype),
        scratch_shapes=[pltpu.SemaphoreType.DMA((2,))],
        compiler_params=pltpu.CompilerParams(vmem_limit_bytes=1024 * 1024),
    )(mine, other, _after)


def dots_kernel(scalars, values, out):
    received, *pairs = values
    grads = jnp.sum(received, axis=0)
    squares = jnp.sum(grads * grads, axis=1, keepdims=True)
    parts = []
    for pair in pairs:
        parts.append(lax.dot_general(
            grads, pair, (((1,), (1,)), ((), ())),
            precision=lax.Precision.HIGHEST, preferred_element_type=jnp.float32,
        ))
    parts.append(jnp.broadcast_to(squares, (4, 128)))
    packed = jnp.concatenate(parts, axis=1)
    out[...] = jnp.broadcast_to(packed[None], out.shape)


def scores_kernel(scalars, values, out):
    group = scalars[0]
    sums = jnp.sum(values[0], axis=0)
    scale = jnp.sqrt(sums[:, 512:640] + 1e-06)
    y, core = group[0] >> 1, group[0] & 1
    for n in range(4):
        part = pltpu.roll(sums[:, n * 128 : (n + 1) * 128], core * 64, 1) / scale
        out[:, pl.ds(pl.multiple_of(((y - n) & 3) * 128, 128), 128)] = part


def per_device(hidden_acts, out_grads, proj_in, proj_out, lengths, val_grads):
    place = lax.axis_index("units").astype(jnp.int32).reshape(1)
    group = lax.axis_index("prompts").astype(jnp.int32).reshape(1)
    smem = pl.BlockSpec(memory_space=pltpu.SMEM)
    other = lax.ppermute(val_grads, "prompts", [(n, n ^ 1) for n in range(8)])
    scal = pl.pallas_call(
        plan_kernel,
        in_specs=[smem] * 2,
        out_specs=smem,
        out_shape=jax.ShapeDtypeStruct((8,), jnp.int32),
    )(lengths, place)
    scal, other = lax.optimization_barrier((scal, other))
    shards = lax.switch(
        scal[6],
        [lambda *ops, tb=tb: reduce_blocks(tb, *ops) for tb in BLOCK_SIZES],
        scal, hidden_acts, out_grads, proj_in.T, proj_out.T,
    )
    received = lax.all_to_all(shards, "units", 0, 0, tiled=True)
    pairs = [pair_up(val_grads, other, shards)]
    for step in (1, 3, 2):
        hops = [(2 * y + c, 2 * ((y + step) % 4) + c) for y in range(4) for c in range(2)]
        pairs.append(lax.ppermute(pairs[0], "prompts", hops))
    pairs = [pairs[0], pairs[1], pairs[3], pairs[2]]
    packed = call_fetching(dots_kernel, (16, 4, 640), [], [received] + pairs)
    return call_fetching(scores_kernel, (4, 512), [group], [lax.all_to_all(packed, "units", 0, 0, tiled=True)])


def solution(mesh):
    in_specs = (
        P("prompts", None, "units"),
        P("prompts", None, "units"),
        P("units", None),
        P("units", None),
        P("prompts"),
        P("prompts", "units"),
    )
    return jax.shard_map(
        per_device, mesh=mesh, in_specs=in_specs, out_specs=P("prompts", None), check_vma=False
    )
```

```python
import jax
import jax.numpy as jnp
from jax import lax
from jax.experimental import pallas as pl
from jax.experimental.pallas import tpu as pltpu
from jax.sharding import PartitionSpec as P

SIDE = 4
PIECES = 2 * SIDE * SIDE
SLOTS = 2048
BLOCK_SIZES = (160, 192, 208, 224, 256)


def blocks_of(scal, p, tb):
    return lax.div(scal[p] + (tb - 1), tb)


def block_ends(scal, tb):
    second = blocks_of(scal, 0, tb)
    third = second + blocks_of(scal, 1, tb)
    fourth = third + blocks_of(scal, 2, tb)
    return second, third, fourth, fourth + blocks_of(scal, 3, tb)


def block_info(scal, tb, ends, m):
    second, third, fourth, end = ends
    prompt = (m >= second).astype(jnp.int32) + (m >= third).astype(jnp.int32) + (m >= fourth).astype(jnp.int32)
    first = jnp.where(m >= fourth, fourth, jnp.where(m >= third, third, jnp.where(m >= second, second, 0)))
    inside = m < end
    token = jnp.where(inside, (m - first) * tb, 0)
    start = jnp.minimum(token, SLOTS - tb)
    high = jnp.where(inside, scal[prompt] - start, 0)
    return prompt, pl.multiple_of(start, 16), token - start, high


def packed_index(scal, h, j, k):
    x, z = scal[4], scal[5]
    major = jnp.where(h == 0, x, z)
    minor = jnp.where(h == 0, z, x)
    return h * (SIDE * SIDE) + ((major + j) & 3) * SIDE + ((minor + k) & 3)


def plan_kernel(lengths, place, out, choice):
    for p in range(4):
        out[p] = lengths[p]
    out[4] = place[0] >> 2
    out[5] = place[0] & 3
    branch = 0
    for tb in BLOCK_SIZES[:-1]:
        blocks = sum(blocks_of(lengths, p, tb) for p in range(4))
        branch = branch + (blocks > PIECES).astype(jnp.int32)
    out[6] = 0
    out[7] = 0
    choice[0] = branch


def project_kernel(tb, steps, scal, acts, grads, w_in, w_out, *refs):
    count = 2 * len(steps)
    outs = refs[:count]
    buf, w_buf, result, bounds, a_sem, g_sem, w_sem, r_sem = refs[count:]
    units = acts.shape[2]
    w_buf[...] = jnp.zeros_like(w_buf)
    weights = [
        pltpu.make_async_copy(w_in, w_buf.at[:64, :units], w_sem.at[0]),
        pltpu.make_async_copy(w_out, w_buf.at[64:, units:], w_sem.at[1]),
    ]
    for copy in weights:
        copy.start()

    def pair(n, k, prompt, start):
        rows = pl.ds(pl.multiple_of(k * tb, 16), tb)
        return (
            pltpu.make_async_copy(acts.at[prompt, pl.ds(start, tb)], buf.at[n, rows, :units], a_sem.at[n]),
            pltpu.make_async_copy(grads.at[prompt, pl.ds(start, tb)], buf.at[n, rows, units:], g_sem.at[n]),
        )

    ends = block_ends(scal, tb)

    def fetch(i, _):
        n, k = i >> 2, i & 3
        j = steps[-1]
        for place, step in enumerate(steps[:-1]):
            j = jnp.where(n >> 1 == place, step, j)
        prompt, start, low, high = block_info(scal, tb, ends, packed_index(scal, n & 1, j, k))
        bounds[i, 0] = low
        bounds[i, 1] = high
        for copy in pair(n, k, prompt, start):
            copy.start()
        return 0

    lax.fori_loop(0, count * SIDE, fetch, 0)
    for copy in weights:
        copy.wait()
    row = lax.broadcasted_iota(jnp.int32, (tb, 128), 0)

    def hand_over(n, act):
        for q in range(count):
            @pl.when(n == q)
            def _():
                act(pltpu.make_async_copy(result.at[q & 1], outs[q], r_sem.at[q & 1]))

    def compute(n, _):
        for k in range(SIDE):
            for copy in pair(n, k, 0, 0):
                copy.wait()
        hand_over(n - 2, lambda copy: copy.wait())
        group = SIDE if tb < SLOTS // 8 else 2

        def part(c, _):
            rows = pl.ds(pl.multiple_of(c * (group * tb), 16), group * tb)
            both = lax.dot_general(
                buf[n, rows], w_buf[...], (((1,), (1,)), ((), ())), preferred_element_type=jnp.float32
            )
            for k in range(group):
                at = c * group + k
                keep = (row >= bounds[n * SIDE + at, 0]) & (row < bounds[n * SIDE + at, 1])
                result[n & 1, at] = jnp.where(keep, both[k * tb : (k + 1) * tb], 0.0)
            return 0

        if group == SIDE:
            part(0, 0)
        else:
            lax.fori_loop(0, SIDE // group, part, 0)
        hand_over(n, lambda copy: copy.start())
        return 0

    lax.fori_loop(0, count, compute, 0)
    for q in range(count - 2, count):
        pltpu.make_async_copy(result.at[q & 1], outs[q], r_sem.at[q & 1]).wait()


def project(tb, steps, scal, acts, grads, w_in, w_out):
    units, width = acts.shape[2], grads.shape[2]
    count = 2 * len(steps)
    rows = count * SIDE * tb
    return pl.pallas_call(
        lambda *refs: project_kernel(tb, steps, *refs),
        in_specs=[pl.BlockSpec(memory_space=pltpu.SMEM)] + [pl.BlockSpec(memory_space=pl.ANY)] * 4,
        out_specs=[pl.BlockSpec(memory_space=pltpu.VMEM)] * count,
        out_shape=[jax.ShapeDtypeStruct((SIDE, tb, 128), jnp.float32)] * count,
        scratch_shapes=[
            pltpu.VMEM((count, SIDE * tb, units + width), jnp.bfloat16),
            pltpu.VMEM((128, units + width), jnp.bfloat16),
            pltpu.VMEM((2, SIDE, tb, 128), jnp.float32),
            pltpu.SMEM((count * SIDE, 2), jnp.int32),
            pltpu.SemaphoreType.DMA((count,)),
            pltpu.SemaphoreType.DMA((count,)),
            pltpu.SemaphoreType.DMA((2,)),
            pltpu.SemaphoreType.DMA((2,)),
        ],
        compiler_params=pltpu.CompilerParams(vmem_limit_bytes=50 * 1024 * 1024),
        cost_estimate=pl.CostEstimate(
            flops=2 * rows * (units + width) * 256,
            bytes_accessed=rows * ((units + width) * 2 + 512),
            transcendentals=0,
        ),
    )(scal, acts, grads, w_in, w_out)


def fetch_all(refs, sems):
    half = len(refs) // 2
    copies = [pltpu.make_async_copy(refs[n], refs[half + n], sems.at[n]) for n in range(half)]
    for copy in copies:
        copy.start()
    for copy in copies:
        copy.wait()
    return [ref[...] for ref in refs[half:]]


def call_fetching(kernel, out_shape, scalars, operands):
    def body(*refs):
        first, last = len(scalars), len(scalars) + len(operands)
        kernel(refs[:first], fetch_all(refs[first:last] + refs[last + 1 : -1], refs[-1]), refs[last])

    return pl.pallas_call(
        body,
        in_specs=[pl.BlockSpec(memory_space=pltpu.SMEM)] * len(scalars) + [pl.BlockSpec(memory_space=pl.ANY)] * len(operands),
        out_specs=pl.BlockSpec(memory_space=pltpu.VMEM),
        out_shape=jax.ShapeDtypeStruct(out_shape, jnp.float32),
        scratch_shapes=[pltpu.VMEM(v.shape, v.dtype) for v in operands] + [pltpu.SemaphoreType.DMA((len(operands),))],
        compiler_params=pltpu.CompilerParams(vmem_limit_bytes=12 * 1024 * 1024),
    )(*scalars, *operands)


def outer_kernel(tb, scalars, values, out):
    scal = scalars[0]
    row = lax.broadcasted_iota(jnp.int32, (64, 64), 0)
    col = lax.broadcasted_iota(jnp.int32, (64, 64), 1)
    order = ((row & 15) * 4 + (row >> 4) == col).astype(jnp.float32)
    each, owner = [], []
    for h in range(2):
        a, b, c, d = values[4 * h : 4 * h + 4]
        rows = (a + b) + (c + d)
        product = lax.dot_general(
            rows[:, :64], rows[:, 64:], (((0,), (0,)), ((), ())),
            precision=lax.Precision.HIGHEST, preferred_element_type=jnp.float32,
        )
        each.append(jnp.dot(order, product, precision=lax.Precision.HIGHEST, preferred_element_type=jnp.float32))
        owner.append(block_info(scal, tb, block_ends(scal, tb), packed_index(scal, h, 0, 0))[0])
    for p in range(4):
        total = jnp.where(owner[0] == p, each[0], 0.0) + jnp.where(owner[1] == p, each[1], 0.0)
        for i in range(4):
            out[:, p, i * 64 : (i + 1) * 64] = total[i * 16 : (i + 1) * 16]


def along(axis, step):
    pairs = []
    for x in range(SIDE):
        for z in range(SIDE):
            if axis == "x":
                pairs.append((x * SIDE + z, (x + step) % SIDE * SIDE + z))
            else:
                pairs.append((x * SIDE + z, x * SIDE + (z + step) % SIDE))
    return pairs


def send(value, axis, step):
    return lax.ppermute(value, "units", along(axis, step))


def reduce_blocks(tb, scal, acts, grads, w_in, w_out):
    x1, z1, x3, z3 = project(tb, (1, 3), scal, acts, grads, w_in, w_out)
    from_x1, from_x3 = send(x1, "x", 1), send(x3, "x", 3)
    from_z1, from_z3 = send(z1, "z", 1), send(z3, "z", 3)
    x2, z2, x0, z0 = project(tb, (2, 0), scal, acts, grads, w_in, w_out)
    sum_x, z2 = lax.optimization_barrier((x0 + (from_x1 + from_x3), z2))
    total_x = sum_x + send(x2, "x", 2)
    total_z = (z0 + (from_z1 + from_z3)) + send(z2, "z", 2)
    final = []
    for total, axis in ((total_x, "z"), (total_z, "x")):
        final.append(total[0])
        final += [send(total[k], axis, k) for k in (2, 1, 3)]
    return call_fetching(lambda *refs: outer_kernel(tb, *refs), (16, 4, 256), [scal], final)


def pair_up(mine, other, _after):
    def body(mine_ref, other_ref, _, out, sems):
        copies = [
            pltpu.make_async_copy(mine_ref, out.at[:64], sems.at[0]),
            pltpu.make_async_copy(other_ref, out.at[64:], sems.at[1]),
        ]
        for copy in copies:
            copy.start()
        for copy in copies:
            copy.wait()

    return pl.pallas_call(
        body,
        in_specs=[pl.BlockSpec(memory_space=pl.ANY)] * 3,
        out_specs=pl.BlockSpec(memory_space=pl.ANY),
        out_shape=jax.ShapeDtypeStruct((128, mine.shape[1]), mine.dtype),
        scratch_shapes=[pltpu.SemaphoreType.DMA((2,))],
        compiler_params=pltpu.CompilerParams(vmem_limit_bytes=1024 * 1024),
    )(mine, other, _after)


def dots_kernel(scalars, values, out):
    received, *pairs = values
    grads = jnp.sum(received, axis=0)
    squares = jnp.sum(grads * grads, axis=1, keepdims=True)
    parts = []
    for pair in pairs:
        parts.append(lax.dot_general(
            grads, pair, (((1,), (1,)), ((), ())),
            precision=lax.Precision.HIGHEST, preferred_element_type=jnp.float32,
        ))
    parts.append(jnp.broadcast_to(squares, (4, 128)))
    packed = jnp.concatenate(parts, axis=1)
    out[...] = jnp.broadcast_to(packed[None], out.shape)


def scores_kernel(scalars, values, out):
    group = scalars[0]
    sums = jnp.sum(values[0], axis=0)
    scale = jnp.sqrt(sums[:, 512:640] + 1e-06)
    y, core = group[0] >> 1, group[0] & 1
    for n in range(4):
        part = pltpu.roll(sums[:, n * 128 : (n + 1) * 128], core * 64, 1) / scale
        out[:, pl.ds(pl.multiple_of(((y - n) & 3) * 128, 128), 128)] = part


def per_device(hidden_acts, out_grads, proj_in, proj_out, lengths, val_grads):
    place = lax.axis_index("units").astype(jnp.int32).reshape(1)
    group = lax.axis_index("prompts").astype(jnp.int32).reshape(1)
    smem = pl.BlockSpec(memory_space=pltpu.SMEM)
    other = lax.ppermute(val_grads, "prompts", [(n, n ^ 1) for n in range(8)])
    scal, choice = pl.pallas_call(
        plan_kernel,
        in_specs=[smem] * 2,
        out_specs=[smem] * 2,
        out_shape=[jax.ShapeDtypeStruct((8,), jnp.int32), jax.ShapeDtypeStruct((1,), jnp.int32)],
    )(lengths, place)
    scal, other = lax.optimization_barrier((scal, other))
    shards = lax.switch(
        choice[0],
        [lambda *ops, tb=tb: reduce_blocks(tb, *ops) for tb in BLOCK_SIZES],
        scal, hidden_acts, out_grads, proj_in.T, proj_out.T,
    )
    received = lax.all_to_all(shards, "units", 0, 0, tiled=True)
    pairs = [pair_up(val_grads, other, shards)]
    for step in (1, 3, 2):
        hops = [(2 * y + c, 2 * ((y + step) % 4) + c) for y in range(4) for c in range(2)]
        pairs.append(lax.ppermute(pairs[0], "prompts", hops))
    pairs = [pairs[0], pairs[1], pairs[3], pairs[2]]
    packed = call_fetching(dots_kernel, (16, 4, 640), [], [received] + pairs)
    return call_fetching(scores_kernel, (4, 512), [group], [lax.all_to_all(packed, "units", 0, 0, tiled=True)])


def solution(mesh):
    in_specs = (
        P("prompts", None, "units"),
        P("prompts", None, "units"),
        P("units", None),
        P("units", None),
        P("prompts"),
        P("prompts", "units"),
    )
    return jax.shard_map(
        per_device, mesh=mesh, in_specs=in_specs, out_specs=P("prompts", None), check_vma=False
    )
```

```python
import jax
import jax.numpy as jnp
from jax import lax
from jax.experimental import pallas as pl
from jax.experimental.pallas import tpu as pltpu
from jax.sharding import PartitionSpec as P

SIDE = 4
PIECES = 2 * SIDE * SIDE
SLOTS = 2048
BLOCK_SIZES = (160, 192, 208, 224, 256)


def blocks_of(scal, p, tb):
    return lax.div(scal[p] + (tb - 1), tb)


def block_ends(scal, tb):
    second = blocks_of(scal, 0, tb)
    third = second + blocks_of(scal, 1, tb)
    fourth = third + blocks_of(scal, 2, tb)
    return second, third, fourth, fourth + blocks_of(scal, 3, tb)


def block_info(scal, tb, ends, m):
    second, third, fourth, end = ends
    prompt = (m >= second).astype(jnp.int32) + (m >= third).astype(jnp.int32) + (m >= fourth).astype(jnp.int32)
    first = jnp.where(m >= fourth, fourth, jnp.where(m >= third, third, jnp.where(m >= second, second, 0)))
    inside = m < end
    token = jnp.where(inside, (m - first) * tb, 0)
    start = jnp.minimum(token, SLOTS - tb)
    high = jnp.where(inside, scal[prompt] - start, 0)
    return prompt, pl.multiple_of(start, 16), token - start, high


def packed_index(scal, h, j, k):
    x, z = scal[4], scal[5]
    major = jnp.where(h == 0, x, z)
    minor = jnp.where(h == 0, z, x)
    return h * (SIDE * SIDE) + ((major + j) & 3) * SIDE + ((minor + k) & 3)


def plan_kernel(lengths, place, out, choice):
    for p in range(4):
        out[p] = lengths[p]
    out[4] = place[0] >> 2
    out[5] = place[0] & 3
    branch = 0
    for tb in BLOCK_SIZES[:-1]:
        blocks = sum(blocks_of(lengths, p, tb) for p in range(4))
        branch = branch + (blocks > PIECES).astype(jnp.int32)
    out[6] = 0
    out[7] = 0
    choice[0] = branch


def project_kernel(tb, steps, scal, acts, grads, w_in, w_out, *refs):
    count = 2 * len(steps)
    outs = refs[:count]
    buf, w_buf, result, bounds, a_sem, g_sem, w_sem, r_sem = refs[count:]
    units = acts.shape[2]
    w_buf[...] = jnp.zeros_like(w_buf)
    weights = [
        pltpu.make_async_copy(w_in, w_buf.at[:64, :units], w_sem.at[0]),
        pltpu.make_async_copy(w_out, w_buf.at[64:, units:], w_sem.at[1]),
    ]
    for copy in weights:
        copy.start()

    def pair(n, k, prompt, start):
        rows = pl.ds(pl.multiple_of(k * tb, 16), tb)
        return (
            pltpu.make_async_copy(acts.at[prompt, pl.ds(start, tb)], buf.at[n, rows, :units], a_sem.at[n]),
            pltpu.make_async_copy(grads.at[prompt, pl.ds(start, tb)], buf.at[n, rows, units:], g_sem.at[n]),
        )

    ends = block_ends(scal, tb)

    def fetch(i, _):
        n, k = i >> 2, i & 3
        j = steps[-1]
        for place, step in enumerate(steps[:-1]):
            j = jnp.where(n >> 1 == place, step, j)
        prompt, start, low, high = block_info(scal, tb, ends, packed_index(scal, n & 1, j, k))
        bounds[i, 0] = low
        bounds[i, 1] = high
        for copy in pair(n, k, prompt, start):
            copy.start()
        return 0

    lax.fori_loop(0, count * SIDE, fetch, 0)
    for copy in weights:
        copy.wait()
    row = lax.broadcasted_iota(jnp.int32, (tb, 128), 0)

    def hand_over(n, act):
        for q in range(count):
            @pl.when(n == q)
            def _():
                act(pltpu.make_async_copy(result.at[q & 1], outs[q], r_sem.at[q & 1]))

    def compute(n, _):
        for k in range(SIDE):
            for copy in pair(n, k, 0, 0):
                copy.wait()
        hand_over(n - 2, lambda copy: copy.wait())
        group = SIDE if tb < SLOTS // 8 else 2

        def part(c, _):
            rows = pl.ds(pl.multiple_of(c * (group * tb), 16), group * tb)
            both = lax.dot_general(
                buf[n, rows], w_buf[...], (((1,), (1,)), ((), ())), preferred_element_type=jnp.float32
            )
            for k in range(group):
                at = c * group + k
                keep = (row >= bounds[n * SIDE + at, 0]) & (row < bounds[n * SIDE + at, 1])
                result[n & 1, at] = jnp.where(keep, both[k * tb : (k + 1) * tb], 0.0)
            return 0

        if group == SIDE:
            part(0, 0)
        else:
            lax.fori_loop(0, SIDE // group, part, 0)
        hand_over(n, lambda copy: copy.start())
        return 0

    lax.fori_loop(0, count, compute, 0)
    for q in range(count - 2, count):
        pltpu.make_async_copy(result.at[q & 1], outs[q], r_sem.at[q & 1]).wait()


def project(tb, steps, scal, acts, grads, w_in, w_out):
    units, width = acts.shape[2], grads.shape[2]
    count = 2 * len(steps)
    rows = count * SIDE * tb
    return pl.pallas_call(
        lambda *refs: project_kernel(tb, steps, *refs),
        in_specs=[pl.BlockSpec(memory_space=pltpu.SMEM)] + [pl.BlockSpec(memory_space=pl.ANY)] * 4,
        out_specs=[pl.BlockSpec(memory_space=pltpu.VMEM)] * count,
        out_shape=[jax.ShapeDtypeStruct((SIDE, tb, 128), jnp.float32)] * count,
        scratch_shapes=[
            pltpu.VMEM((count, SIDE * tb, units + width), jnp.bfloat16),
            pltpu.VMEM((128, units + width), jnp.bfloat16),
            pltpu.VMEM((2, SIDE, tb, 128), jnp.float32),
            pltpu.SMEM((count * SIDE, 2), jnp.int32),
            pltpu.SemaphoreType.DMA((count,)),
            pltpu.SemaphoreType.DMA((count,)),
            pltpu.SemaphoreType.DMA((2,)),
            pltpu.SemaphoreType.DMA((2,)),
        ],
        compiler_params=pltpu.CompilerParams(vmem_limit_bytes=50 * 1024 * 1024),
        cost_estimate=pl.CostEstimate(
            flops=2 * rows * (units + width) * 256,
            bytes_accessed=rows * ((units + width) * 2 + 512),
            transcendentals=0,
        ),
    )(scal, acts, grads, w_in, w_out)


def fetch_all(refs, sems):
    half = len(refs) // 2
    copies = [pltpu.make_async_copy(refs[n], refs[half + n], sems.at[n]) for n in range(half)]
    for copy in copies:
        copy.start()
    for copy in copies:
        copy.wait()
    return [ref[...] for ref in refs[half:]]


def call_fetching(kernel, out_shape, scalars, operands):
    def body(*refs):
        first, last = len(scalars), len(scalars) + len(operands)
        kernel(refs[:first], fetch_all(refs[first:last] + refs[last + 1 : -1], refs[-1]), refs[last])

    return pl.pallas_call(
        body,
        in_specs=[pl.BlockSpec(memory_space=pltpu.SMEM)] * len(scalars) + [pl.BlockSpec(memory_space=pl.ANY)] * len(operands),
        out_specs=pl.BlockSpec(memory_space=pltpu.VMEM),
        out_shape=jax.ShapeDtypeStruct(out_shape, jnp.float32),
        scratch_shapes=[pltpu.VMEM(v.shape, v.dtype) for v in operands] + [pltpu.SemaphoreType.DMA((len(operands),))],
        compiler_params=pltpu.CompilerParams(vmem_limit_bytes=12 * 1024 * 1024),
    )(*scalars, *operands)


def outer_kernel(tb, scalars, values, out):
    scal = scalars[0]
    row = lax.broadcasted_iota(jnp.int32, (64, 64), 0)
    col = lax.broadcasted_iota(jnp.int32, (64, 64), 1)
    order = ((row & 15) * 4 + (row >> 4) == col).astype(jnp.float32)
    each, owner = [], []
    for h in range(2):
        a, b, c, d = values[4 * h : 4 * h + 4]
        rows = (a + b) + (c + d)
        product = lax.dot_general(
            rows[:, :64], rows[:, 64:], (((0,), (0,)), ((), ())),
            precision=lax.Precision.HIGHEST, preferred_element_type=jnp.float32,
        )
        each.append(product)
        owner.append(block_info(scal, tb, block_ends(scal, tb), packed_index(scal, h, 0, 0))[0])
    lane = lax.broadcasted_iota(jnp.int32, (64, 128), 1)
    both = jnp.dot(order, jnp.concatenate(each, axis=1), precision=lax.Precision.HIGHEST, preferred_element_type=jnp.float32)
    for p in range(4):
        kept = jnp.where(jnp.where(lane < 64, owner[0], owner[1]) == p, both, 0.0)
        total = kept[:, :64] + kept[:, 64:]
        for i in range(4):
            out[:, p, i * 64 : (i + 1) * 64] = total[i * 16 : (i + 1) * 16]


def along(axis, step):
    pairs = []
    for x in range(SIDE):
        for z in range(SIDE):
            if axis == "x":
                pairs.append((x * SIDE + z, (x + step) % SIDE * SIDE + z))
            else:
                pairs.append((x * SIDE + z, x * SIDE + (z + step) % SIDE))
    return pairs


def send(value, axis, step):
    return lax.ppermute(value, "units", along(axis, step))


def reduce_blocks(tb, scal, acts, grads, w_in, w_out):
    x1, z1, x3, z3 = project(tb, (1, 3), scal, acts, grads, w_in, w_out)
    from_x1, from_x3 = send(x1, "x", 1), send(x3, "x", 3)
    from_z1, from_z3 = send(z1, "z", 1), send(z3, "z", 3)
    x2, z2, x0, z0 = project(tb, (2, 0), scal, acts, grads, w_in, w_out)
    sum_x, z2 = lax.optimization_barrier((x0 + (from_x1 + from_x3), z2))
    total_x = sum_x + send(x2, "x", 2)
    total_z = (z0 + (from_z1 + from_z3)) + send(z2, "z", 2)
    final = []
    for total, axis in ((total_x, "z"), (total_z, "x")):
        final.append(total[0])
        final += [send(total[k], axis, k) for k in (2, 1, 3)]
    return call_fetching(lambda *refs: outer_kernel(tb, *refs), (16, 4, 256), [scal], final)


def pair_up(mine, other, _after):
    def body(mine_ref, other_ref, _, out, sems):
        copies = [
            pltpu.make_async_copy(mine_ref, out.at[:64], sems.at[0]),
            pltpu.make_async_copy(other_ref, out.at[64:], sems.at[1]),
        ]
        for copy in copies:
            copy.start()
        for copy in copies:
            copy.wait()

    return pl.pallas_call(
        body,
        in_specs=[pl.BlockSpec(memory_space=pl.ANY)] * 3,
        out_specs=pl.BlockSpec(memory_space=pl.ANY),
        out_shape=jax.ShapeDtypeStruct((128, mine.shape[1]), mine.dtype),
        scratch_shapes=[pltpu.SemaphoreType.DMA((2,))],
        compiler_params=pltpu.CompilerParams(vmem_limit_bytes=1024 * 1024),
    )(mine, other, _after)


def dots_kernel(scalars, values, out):
    received, *pairs = values
    grads = jnp.sum(received, axis=0)
    squares = jnp.sum(grads * grads, axis=1, keepdims=True)
    parts = []
    for pair in pairs:
        parts.append(lax.dot_general(
            grads, pair, (((1,), (1,)), ((), ())),
            precision=lax.Precision.HIGHEST, preferred_element_type=jnp.float32,
        ))
    parts.append(jnp.broadcast_to(squares, (4, 128)))
    packed = jnp.concatenate(parts, axis=1)
    out[...] = jnp.broadcast_to(packed[None], out.shape)


def scores_kernel(scalars, values, out):
    group = scalars[0]
    sums = jnp.sum(values[0], axis=0)
    scale = jnp.sqrt(sums[:, 512:640] + 1e-06)
    y, core = group[0] >> 1, group[0] & 1
    for n in range(4):
        part = pltpu.roll(sums[:, n * 128 : (n + 1) * 128], core * 64, 1) / scale
        out[:, pl.ds(pl.multiple_of(((y - n) & 3) * 128, 128), 128)] = part


def per_device(hidden_acts, out_grads, proj_in, proj_out, lengths, val_grads):
    place = lax.axis_index("units").astype(jnp.int32).reshape(1)
    group = lax.axis_index("prompts").astype(jnp.int32).reshape(1)
    smem = pl.BlockSpec(memory_space=pltpu.SMEM)
    other = lax.ppermute(val_grads, "prompts", [(n, n ^ 1) for n in range(8)])
    scal, choice = pl.pallas_call(
        plan_kernel,
        in_specs=[smem] * 2,
        out_specs=[smem] * 2,
        out_shape=[jax.ShapeDtypeStruct((8,), jnp.int32), jax.ShapeDtypeStruct((1,), jnp.int32)],
    )(lengths, place)
    scal, other = lax.optimization_barrier((scal, other))
    shards = lax.switch(
        choice[0],
        [lambda *ops, tb=tb: reduce_blocks(tb, *ops) for tb in BLOCK_SIZES],
        scal, hidden_acts, out_grads, proj_in.T, proj_out.T,
    )
    received = lax.all_to_all(shards, "units", 0, 0, tiled=True)
    pairs = [pair_up(val_grads, other, shards)]
    for step in (1, 3, 2):
        hops = [(2 * y + c, 2 * ((y + step) % 4) + c) for y in range(4) for c in range(2)]
        pairs.append(lax.ppermute(pairs[0], "prompts", hops))
    pairs = [pairs[0], pairs[1], pairs[3], pairs[2]]
    packed = call_fetching(dots_kernel, (16, 4, 640), [], [received] + pairs)
    return call_fetching(scores_kernel, (4, 512), [group], [lax.all_to_all(packed, "units", 0, 0, tiled=True)])


def solution(mesh):
    in_specs = (
        P("prompts", None, "units"),
        P("prompts", None, "units"),
        P("units", None),
        P("units", None),
        P("prompts"),
        P("prompts", "units"),
    )
    return jax.shard_map(
        per_device, mesh=mesh, in_specs=in_specs, out_specs=P("prompts", None), check_vma=False
    )
```
